256 devices in a mesh: blk: 32 (over z_hi, y, core), slab: 8 (over x, z_lo).
Axes of the slice: x: 4, y: 4, z: 8 (z_hi: 4, z_lo: 2; z = z_hi * 2 + z_lo), core: 2. Of those that a mesh axis runs over, the one named last changes fastest.
Arguments:
- interactions: bfloat16 [7040, 65536], P('slab', 'blk'), may hold values from -6 to 6
- user_weight: float32 [7040], P('slab'), may hold values from 0.25 to 4
Outputs:
- gram_tiles: float32 [2, 65536, 2048], P(None, ('blk', 'slab'))
The draws below stay inside these ranges and needn't reach their ends.
All inputs are finite; a program needn't handle non-finite values.
Results may differ from the reference program's by a relative error of at most 0.015.
Values may be sent and summed in bfloat16 or wider, within the bound.
A program may use at most 128 MiB of HBM per device.

```python
import math
import jax
import jax.numpy as jnp
from jax import lax

BLK = 2048
U_DEV = 880
ROUNDS = 2
ITEMS = 65536
USERS = 7040
N_SLAB = 8


def levels(rng, dims, split, smallest, high):
    def one(axis_at, blocks):
        draws = jax.random.uniform(jax.random.fold_in(jax.random.fold_in(rng, 6), axis_at), (blocks,), jnp.float32, smallest / len(split), high / len(split))
        return jnp.repeat(jnp.exp(draws), dims[axis_at] // blocks).reshape((-1,) + (1,) * (len(dims) - axis_at - 1))

    gain = one(*split[0])
    for cut in split[1:]:
        gain = gain * one(*cut)
    return gain


def normal_values(rng, shape, width, reach, pieces=(), held_as=jnp.bfloat16):
    level = levels(rng, shape, pieces, -0.22, 0.18) if pieces else 1.0
    values = jax.random.normal(rng, shape, jnp.float32) * width * level
    return jnp.minimum(jnp.maximum(values, -reach), reach).astype(held_as)


def setup_inputs(seed: int = 0) -> dict:
    streams_of = jax.random.split(jax.random.key(seed), 3)
    interactions = normal_values(streams_of[0], (USERS, ITEMS), 1.0, 6.0, ((0, 8), (1, 32)))
    user_weight = jnp.clip(jnp.exp(math.log(4.0) - 2.7725887 * jax.random.uniform(streams_of[1], (USERS,), jnp.float32) ** levels(streams_of[1], (USERS,), ((0, 8),), -0.2, 0.2)), 0.25, 4.0)
    return dict(interactions=interactions, user_weight=user_weight)


def reference(interactions, user_weight):
    scale = 1.0 / jnp.sqrt(jnp.float32(USERS))
    weighted = (interactions.astype(jnp.float32) * user_weight[:, None] * scale).astype(jnp.bfloat16)
    nblocks = ITEMS // BLK
    zblocks = weighted.reshape(N_SLAB, U_DEV, nblocks, BLK).transpose(2, 0, 1, 3)
    xblocks = interactions.reshape(N_SLAB, U_DEV, nblocks, BLK).transpose(2, 0, 1, 3)
    results = []
    for step in range(ROUNDS):
        partner = jnp.roll(xblocks, -(step + 1), axis=0)

        def one_tile(pair):
            left, right = pair
            part = jnp.einsum('sui,suj->sij', left.astype(jnp.float32), right.astype(jnp.float32))
            rounded = lax.optimization_barrier(part.astype(jnp.bfloat16))
            return lax.optimization_barrier(jnp.sum(rounded.astype(jnp.float32), axis=0))
        tiles = lax.map(one_tile, (zblocks, partner))
        results.append(tiles.reshape(ITEMS, BLK))
    return jnp.stack(results)
```

```python
import functools

import jax
import jax.numpy as jnp
from jax import lax
from jax.experimental import pallas as pl
from jax.experimental.pallas import tpu as pltpu
from jax.sharding import PartitionSpec as P

ROUNDS = 2
CHUNKS = 4
RING = 4
PADDED = 896
RELAYED = (1, 3)
MESH = pl.DeviceIdType.MESH


def kernel(
    x_ref,
    weight_ref,
    out_ref,
    own,
    weighted,
    partner,
    relay,
    first_out,
    first_in,
    second_out,
    second_in,
    pair_out,
    pair_in,
    total,
    load_sem,
    block_send,
    block_recv,
    relay_recv,
    first_send,
    first_recv,
    second_send,
    second_recv,
    pair_send,
    pair_recv,
    store_sem,
):
    blk, slab = lax.axis_index("blk"), lax.axis_index("slab")
    blocks = lax.axis_size("blk")
    core, y = lax.rem(blk, 2), lax.rem(blk // 2, 4)
    x, z_lo = slab // 2, lax.rem(slab, 2)
    users = x_ref.shape[0]
    width = x_ref.shape[1] // CHUNKS
    rows = x_ref.shape[1] // RING
    half = rows // 2
    units = ROUNDS * CHUNKS
    seconds = core == 1

    right = (blk, lax.rem(x + 1, RING) * 2 + z_lo)
    left = (blk, lax.rem(x + RING - 1, RING) * 2 + z_lo)
    mate = (blk, x * 2 + 1 - z_lo)
    twin = (blk + 1 - 2 * core, slab)
    back = lax.rem(blk + blocks - 2 - core, blocks) + 1
    before = (back, slab)
    front = lax.rem(blk - core + 2, blocks)
    after = ((front, slab), (front + 1, slab))
    relay_at = (blk - core + 7, slab)
    relay_from = ((blk - core - 6, slab), (blk - core - 5, slab))
    relay_to = (lax.rem(blk - core + blocks - 8, blocks) + 1, slab)
    relay_after = (lax.rem(blk - core + 8, blocks) + 1, slab)

    loads = [
        pltpu.make_async_copy(
            x_ref.at[:, pl.ds(j * width, width)], own.at[j, pl.ds(0, users)], load_sem.at[j]
        )
        for j in range(CHUNKS)
    ]
    for load in loads:
        load.start()

    barrier = pltpu.get_barrier_semaphore()

    def greet(device):
        pl.semaphore_signal(barrier, inc=1, device_id=device, device_id_type=MESH)

    for device in (right, left, mate, twin):
        greet(device)

    @pl.when(seconds)
    def _():
        greet(after[0])
        greet(after[1])

    @pl.when(seconds & (y == 3))
    def _():
        greet(relay_from[0])
        greet(relay_from[1])
        greet(relay_after)

    own[:, pl.ds(users, PADDED - users), :] = jnp.zeros(
        (CHUNKS, PADDED - users, width), own.dtype
    )
    partner[:, pl.ds(users, PADDED - users), :] = jnp.zeros(
        (units, PADDED - users, width), partner.dtype
    )
    relays = jnp.where((y == 0) | (seconds & (y == 3)), 1, 0)
    pl.semaphore_wait(barrier, 5 + relays)

    def send(source, target, sent, landed, device):
        return pltpu.make_async_remote_copy(
            src_ref=source,
            dst_ref=target,
            send_sem=sent,
            recv_sem=landed,
            device_id=device,
            device_id_type=MESH,
        )

    def block(ref, at):
        return ref.at[at, pl.ds(0, users)]

    def pass_on(j, unit, sent):
        def direct():
            send(block(own, j), block(partner, unit), sent, block_recv.at[unit], before).start()

        if j in RELAYED:
            slot = unit // CHUNKS * len(RELAYED) + RELAYED.index(j)

            @pl.when(y == 0)
            def _():
                send(block(own, j), relay.at[slot], sent, relay_recv.at[slot], relay_at).start()

            @pl.when(y != 0)
            def _():
                direct()
        else:
            direct()

    def relay_on(slot):
        unit = slot // len(RELAYED) * CHUNKS + RELAYED[slot % len(RELAYED)]
        copy = send(
            relay.at[slot],
            block(partner, unit),
            block_send.at[12 + slot],
            block_recv.at[unit],
            relay_to,
        )
        send(
            relay.at[slot], relay.at[slot], block_send.at[12 + slot], relay_recv.at[slot], relay_to
        ).wait_recv()
        copy.start()

    for j in range(CHUNKS):
        loads[j].wait()

        @pl.when(core == 0)
        def _():
            pass_on(j, j, block_send.at[j])

        @pl.when(seconds)
        def _():
            send(
                block(own, j), block(partner, j), block_send.at[j], block_recv.at[j], twin
            ).start()

    def weigh(step):
        values = own[lax.rem(x + step, RING)].astype(jnp.float32)
        weighted[step] = (values.T * weight_ref[0:1, :] * weight_ref[1:2, :]).astype(
            weighted.dtype
        )

    def gram(step, unit, start, count):
        return jnp.dot(
            weighted[step, pl.ds(start, count)],
            partner[unit],
            preferred_element_type=jnp.float32,
        )

    weigh(2)

    @pl.when(seconds & (y == 3))
    def _():
        relay_on(0)

    def first_copy(unit, way):
        return send(
            first_out.at[unit, way],
            first_in.at[unit, way],
            first_send.at[way, unit],
            first_recv.at[way, unit],
            (right, left)[way],
        )

    def second_copy(unit, way):
        return send(
            second_out.at[unit, way],
            second_in.at[unit, way],
            second_send.at[way, unit],
            second_recv.at[way, unit],
            (right, left)[way],
        )

    def pair_copy(unit):
        return send(
            pair_out.at[unit], pair_in.at[unit], pair_send.at[unit], pair_recv.at[unit], mate
        )

    def store(unit):
        column = pl.multiple_of(lax.rem(unit, CHUNKS) * width, width)
        return pltpu.make_async_copy(
            total.at[unit],
            out_ref.at[unit // CHUNKS, :, pl.ds(column, width)],
            store_sem.at[unit],
        )

    def forward(unit):
        return send(
            block(partner, unit),
            block(partner, unit + CHUNKS),
            block_send.at[8 + unit],
            block_recv.at[unit + CHUNKS],
            twin,
        )

    def step(t, carry):
        @pl.when(t < units)
        def _():
            unit = t
            send(
                block(partner, unit),
                block(partner, unit),
                block_send.at[0],
                block_recv.at[unit],
                twin,
            ).wait_recv()

            @pl.when(seconds & (t < CHUNKS))
            def _():
                forward(unit).start()

            for part in range(2):
                first_out[unit, part] = gram(2, unit, part * half, half).astype(first_out.dtype)
                first_copy(unit, part).start()

            @pl.when(t == 0)
            def _():
                weigh(1)
                weigh(3)
                weigh(0)

            @pl.when(seconds & (y == 3))
            def _():
                for slot, at in ((1, 0), (2, 2), (3, 3)):

                    @pl.when(t == at)
                    def _():
                        relay_on(slot)

            for j in range(CHUNKS):

                @pl.when(seconds & (t == 1 + j // 2))
                def _():
                    pass_on(j, CHUNKS + j, block_send.at[CHUNKS + j])

        @pl.when((t >= 1) & (t < units + 1))
        def _():
            unit = t - 1
            for way in range(2):
                toward = (1, 3)[way]
                first_copy(unit, way).wait_recv()
                merged = gram(toward, unit, way * half, half) + first_in[unit, way].astype(
                    jnp.float32
                )
                second_out[unit, way, way] = merged.astype(second_out.dtype)
                second_out[unit, way, 1 - way] = gram(
                    toward, unit, (1 - way) * half, half
                ).astype(second_out.dtype)
                second_copy(unit, way).start()

        @pl.when((t >= 2) & (t < units + 2))
        def _():
            unit = t - 2
            for way in range(2):
                second_copy(unit, way).wait_recv()

            def gathered(part):
                start = pl.multiple_of(part * half, half)
                return (
                    gram(0, unit, start, half)
                    + second_in[unit, 0, part].astype(jnp.float32)
                    + second_in[unit, 1, part].astype(jnp.float32)
                )

            pair_out[unit] = gathered(1 - z_lo).astype(pair_out.dtype)
            pair_copy(unit).start()
            total[unit] = gathered(z_lo)

        @pl.when(t >= 3)
        def _():
            unit = t - 3
            pair_copy(unit).wait_recv()
            total[unit] = total[unit] + pair_in[unit].astype(jnp.float32)
            store(unit).start()

        return carry

    lax.fori_loop(0, units + 3, step, 0)

    def finish(unit, carry):
        for way in range(2):
            first_copy(unit, way).wait_send()
            second_copy(unit, way).wait_send()
        pair_copy(unit).wait_send()
        store(unit).wait()
        return carry

    lax.fori_loop(0, units, finish, 0)

    def sent(at):
        send(
            block(own, 0), block(partner, 0), block_send.at[at], block_recv.at[0], twin
        ).wait_send()

    for j in range(CHUNKS):
        sent(j)

        @pl.when(seconds)
        def _():
            sent(CHUNKS + j)
            sent(2 * CHUNKS + j)

    @pl.when(seconds & (y == 3))
    def _():
        for slot in range(2 * len(RELAYED)):
            sent(12 + slot)


def on_device(interactions, user_weight):
    users, items = interactions.shape
    slabs = lax.axis_size("slab")
    scale = 1.0 / jnp.sqrt(jnp.float32(users * slabs))
    weights = jnp.stack(
        [jnp.pad(user_weight, (0, PADDED - users)), jnp.full((PADDED,), scale, jnp.float32)]
    )
    width, rows = items // CHUNKS, items // RING
    half = rows // 2
    units = ROUNDS * CHUNKS
    half_type = interactions.dtype
    dma = pltpu.SemaphoreType.DMA
    return pl.pallas_call(
        kernel,
        name="gram_tiles",
        out_shape=jax.ShapeDtypeStruct((ROUNDS, items // slabs, items), jnp.float32),
        in_specs=[
            pl.BlockSpec(memory_space=pl.ANY),
            pl.BlockSpec(memory_space=pltpu.VMEM),
        ],
        out_specs=pl.BlockSpec(memory_space=pl.ANY),
        scratch_shapes=[
            pltpu.VMEM((CHUNKS, PADDED, width), half_type),
            pltpu.VMEM((RING, rows, PADDED), half_type),
            pltpu.VMEM((units, PADDED, width), half_type),
            pltpu.VMEM((ROUNDS * len(RELAYED), users, width), half_type),
            pltpu.VMEM((units, 2, half, width), half_type),
            pltpu.VMEM((units, 2, half, width), half_type),
            pltpu.VMEM((units, 2, 2, half, width), half_type),
            pltpu.VMEM((units, 2, 2, half, width), half_type),
            pltpu.VMEM((units, half, width), half_type),
            pltpu.VMEM((units, half, width), half_type),
            pltpu.VMEM((units, half, width), jnp.float32),
            dma((CHUNKS,)),
            dma((16,)),
            dma((units,)),
            dma((ROUNDS * len(RELAYED),)),
            dma((2, units)),
            dma((2, units)),
            dma((2, units)),
            dma((2, units)),
            dma((units,)),
            dma((units,)),
            dma((units,)),
        ],
        compiler_params=pltpu.CompilerParams(
            collective_id=0, has_side_effects=True, vmem_limit_bytes=60 << 20
        ),
        cost_estimate=pl.CostEstimate(
            flops=ROUNDS * 2 * items * items * users,
            bytes_accessed=users * items * 2 + ROUNDS * items // slabs * items * 4,
            transcendentals=0,
        ),
    )(interactions, weights)


def solution(mesh):
    in_specs = (P("slab", "blk"), P("slab"))
    out_specs = P(None, ("blk", "slab"), None)
    return jax.shard_map(
        on_device, mesh=mesh, in_specs=in_specs, out_specs=out_specs, check_vma=False
    )
```

```python
import functools

import jax
import jax.numpy as jnp
from jax import lax
from jax.experimental import pallas as pl
from jax.experimental.pallas import tpu as pltpu
from jax.sharding import PartitionSpec as P

ROUNDS = 2
CHUNKS = 8
RING = 4
PADDED = 896
PAIR_FIRST = (((), ()), ((5, 7, 9, 11), (4, 6, 8, 10, 12)))
EARLY = max(len(of) for halves in PAIR_FIRST for of in halves)
LAG = 4
STAGES = (1, 3, 5)
ITERATIONS = max([ROUNDS * CHUNKS + STAGES[2]] + [u + LAG + STAGES[1] + 1 for halves in PAIR_FIRST for of in halves for u in of])
PASS_AT = (3, 3, 3, 4, 5, 5, 5, 6)
RELAY_AT = {1: (0, 2, 6, 10), 2: (1, 3, 6, 10), 3: (-1, 1, 6, 10)}
MESH = pl.DeviceIdType.MESH


def kernel(
    x_ref,
    weight_ref,
    out_ref,
    own,
    weighted,
    partner,
    relay,
    first_out,
    first_in,
    second_out,
    second_in,
    pair_out,
    pair_in,
    early_out,
    early_in,
    total,
    load_sem,
    block_send,
    block_recv,
    relay_recv,
    first_send,
    first_recv,
    second_send,
    second_recv,
    pair_send,
    pair_recv,
    early_send,
    early_recv,
    store_sem,
):
    blk, slab = lax.axis_index("blk"), lax.axis_index("slab")
    blocks = lax.axis_size("blk")
    core, y = lax.rem(blk, 2), lax.rem(blk // 2, 4)
    x, z_lo = slab // 2, lax.rem(slab, 2)
    users = x_ref.shape[0]
    width = x_ref.shape[1] // CHUNKS
    rows = x_ref.shape[1] // RING
    half = rows // 2
    quarter = half // 2
    units = ROUNDS * CHUNKS
    seconds = core == 1

    right = (blk, lax.rem(x + 1, RING) * 2 + z_lo)
    left = (blk, lax.rem(x + RING - 1, RING) * 2 + z_lo)
    mate = (blk, x * 2 + 1 - z_lo)
    twin = (blk + 1 - 2 * core, slab)
    back = lax.rem(blk + blocks - 2 - core, blocks) + 1
    before = (back, slab)
    front = lax.rem(blk - core + 2, blocks)
    after = ((front, slab), (front + 1, slab))
    base = blk - lax.rem(blk, 8)
    relay_at = [(base + 2 * at + 1 - core, slab) for at in (3, 1, 2)]
    relay_from = (base + 1 - core, slab)
    relay_to = (lax.rem(base + blocks - 8, blocks) + 7, slab)
    relay_after = [(lax.rem(base + 8, blocks) + at, slab) for at in range(2, 8)]

    loads = [
        pltpu.make_async_copy(
            x_ref.at[:, pl.ds(j * width, width)], own.at[j, pl.ds(0, users)], load_sem.at[j]
        )
        for j in range(CHUNKS)
    ]
    for load in loads:
        load.start()

    barrier = pltpu.get_barrier_semaphore()

    def greet(device):
        pl.semaphore_signal(barrier, inc=1, device_id=device, device_id_type=MESH)

    for device in (right, left, mate, twin):
        greet(device)

    @pl.when(seconds)
    def _():
        greet(after[0])
        greet(after[1])

    @pl.when(y != 0)
    def _():
        greet(relay_from)

    @pl.when(seconds & (y == 3))
    def _():
        for device in relay_after:
            greet(device)

    own[:, pl.ds(users, PADDED - users), :] = jnp.zeros(
        (CHUNKS, PADDED - users, width), own.dtype
    )
    early_in[early_in.shape[0] - 1] = jnp.zeros((half, width), early_in.dtype)
    partner[:, pl.ds(users, PADDED - users), :] = jnp.zeros(
        (units, PADDED - users, width), partner.dtype
    )
    relays = jnp.where(y == 0, 3, 1)
    pl.semaphore_wait(barrier, 5 + relays)

    def send(source, target, sent, landed, device):
        return pltpu.make_async_remote_copy(
            src_ref=source,
            dst_ref=target,
            send_sem=sent,
            recv_sem=landed,
            device_id=device,
            device_id_type=MESH,
        )

    def block(ref, at):
        return ref.at[at, pl.ds(0, users)]

    def pass_on(j, unit, sent):
        def direct():
            send(block(own, j), block(partner, unit), sent, block_recv.at[unit], before).start()

        if j % 4 == 0:
            direct()
        else:
            slot = unit // 4

            @pl.when(y == 0)
            def _():
                send(
                    block(own, j), relay.at[slot], sent, relay_recv.at[slot], relay_at[j % 4 - 1]
                ).start()

            @pl.when(y != 0)
            def _():
                direct()

    def relay_on(slot):
        unit = slot * 4 + lax.rem(y, 3) + 1
        sent = block_send.at[3 * CHUNKS + slot]
        send(relay.at[slot], relay.at[slot], sent, relay_recv.at[slot], relay_to).wait_recv()
        send(relay.at[slot], block(partner, unit), sent, block_recv.at[unit], relay_to).start()

    for j in range(CHUNKS):
        loads[j].wait()

        @pl.when(core == 0)
        def _():
            pass_on(j, j, block_send.at[j])

        @pl.when(seconds)
        def _():
            send(
                block(own, j), block(partner, j), block_send.at[j], block_recv.at[j], twin
            ).start()

    def weigh(step):
        for piece in range(rows // width):
            values = own[lax.rem(x + step, RING) * (rows // width) + piece].T.astype(jnp.float32)
            weighted[step, pl.ds(piece * width, width)] = (
                values * weight_ref[0:1, :] * weight_ref[1:2, :]
            ).astype(weighted.dtype)

    def weigh_rest():
        for step in (1, 3, 0):
            weigh(step)

    def gram(step, unit, part):
        start = pl.multiple_of(part * half, half)
        return jnp.dot(
            weighted[step, pl.ds(start, half)],
            partner[unit],
            preferred_element_type=jnp.float32,
        )

    weigh(2)

    @pl.when(seconds)
    def _():
        weigh_rest()

    def pair_first(unit, part):
        def among(of):
            return functools.reduce(jnp.logical_or, [unit == u for u in of], unit < 0)

        at = [[among(of) for of in halves] for halves in PAIR_FIRST]
        return jnp.where(
            core == 0,
            jnp.where(part == 0, at[0][0], at[0][1]),
            jnp.where(part == 0, at[1][0], at[1][1]),
        )

    def relay_steps(t):
        for slot in range(units // 4):
            at = jnp.where(y == 1, RELAY_AT[1][slot], jnp.where(y == 2, RELAY_AT[2][slot], RELAY_AT[3][slot]))

            @pl.when((core == 1 - slot // (CHUNKS // 4)) & (y != 0) & (t == at))
            def _():
                relay_on(slot)

    def first_copy(job, way):
        return send(
            first_out.at[job, way],
            first_in.at[job, way],
            first_send.at[way, job],
            first_recv.at[way, job],
            (right, left)[way],
        )

    def second_copy(job, way):
        return send(
            second_out.at[job, way],
            second_in.at[job, way],
            second_send.at[way, job],
            second_recv.at[way, job],
            (right, left)[way],
        )

    def pair_copy(unit):
        return send(
            pair_out.at[unit], pair_in.at[unit], pair_send.at[unit], pair_recv.at[unit], mate
        )

    def early_copy(at):
        return send(
            early_out.at[at], early_in.at[at], early_send.at[at], early_recv.at[at], mate
        )

    def early_at(unit, step, part):
        before = [[sum([jnp.where(unit > u, 1, 0) for u in of]) for of in halves] for halves in PAIR_FIRST]
        at = jnp.where(
            core == 0,
            jnp.where(part == 0, before[0][0], before[0][1]),
            jnp.where(part == 0, before[1][0], before[1][1]),
        )
        return at * RING + step

    def store(unit):
        column = pl.multiple_of(lax.rem(unit, CHUNKS) * width, width)
        return pltpu.make_async_copy(
            total.at[unit],
            out_ref.at[unit // CHUNKS, :, pl.ds(column, width)],
            store_sem.at[unit],
        )

    def forward(unit):
        return send(
            block(partner, unit),
            block(partner, unit + CHUNKS),
            block_send.at[2 * CHUNKS + unit],
            block_recv.at[unit + CHUNKS],
            twin,
        )

    def job_of(kind, stage):
        late = kind == 2
        unit = stage - jnp.where(late, LAG, 0)
        mine = jnp.where(kind > 0, 1, 0)
        part = jnp.where(kind > 0, z_lo, 1 - z_lo)
        active = (unit >= 0) & (unit < units) & (pair_first(unit, part) == late)
        return late, unit, mine, part, active

    def each_kind(stage, work):
        def one(kind, carry):
            late, unit, mine, part, active = job_of(kind, stage)

            @pl.when(active)
            def _():
                work(late, unit, mine, part, unit * 2 + mine)

            return carry

        lax.fori_loop(0, 3, one, 0)

    def paired(late, unit, step, part):
        at = jnp.where(late, early_at(unit, step, part), early_in.shape[0] - 1)

        @pl.when(late)
        def _():
            early_copy(at).wait_recv()

        return gram(step, unit, part) + early_in[at].astype(jnp.float32)

    def first_step(late, unit, mine, part, job):
        value = paired(late, unit, 2, part).astype(first_out.dtype)
        for way in range(2):
            first_out[job, way] = value[way * quarter : (way + 1) * quarter]
            first_copy(job, way).start()

    def second_step(late, unit, mine, part, job):
        for way in range(2):
            value = paired(late, unit, (1, 3)[way], part)
            first_copy(job, way).wait_recv()
            joined = slice(way * quarter, (way + 1) * quarter)
            plain = slice((1 - way) * quarter, (2 - way) * quarter)
            second_out[job, way, joined] = (
                value[joined] + first_in[job, way].astype(jnp.float32)
            ).astype(second_out.dtype)
            second_out[job, way, plain] = value[plain].astype(second_out.dtype)
            second_copy(job, way).start()

    def third_step(late, unit, mine, part, job):
        value = paired(late, unit, 0, part)
        for way in range(2):
            second_copy(job, way).wait_recv()
        value = (
            value
            + second_in[job, 0].astype(jnp.float32)
            + second_in[job, 1].astype(jnp.float32)
        )

        @pl.when(mine == 0)
        def _():
            pair_out[unit] = value.astype(pair_out.dtype)
            pair_copy(unit).start()

        @pl.when(mine == 1)
        def _():
            total[unit] = value

        @pl.when(late)
        def _():
            store(unit).start()

    def last_step(unit):
        pair_copy(unit).wait_recv()
        total[unit] = total[unit] + pair_in[unit].astype(jnp.float32)
        store(unit).start()

    def step(t, carry):
        @pl.when(t < units)
        def _():
            send(
                block(partner, t), block(partner, t), block_send.at[0], block_recv.at[t], twin
            ).wait_recv()

            @pl.when(seconds & (t < CHUNKS))
            def _():
                forward(t).start()

            @pl.when(pair_first(t, 1 - z_lo))
            def _():
                def early(i, carry):
                    toward = lax.rem(i + 2, RING)
                    at = early_at(t, toward, 1 - z_lo)
                    early_out[at] = gram(toward, t, 1 - z_lo).astype(early_out.dtype)
                    early_copy(at).start()
                    return carry

                lax.fori_loop(0, RING, early, 0)

        each_kind(t, first_step)

        @pl.when((core == 0) & (t == 0))
        def _():
            weigh_rest()

        for j in range(CHUNKS):

            @pl.when(seconds & (t == PASS_AT[j]))
            def _():
                pass_on(j, CHUNKS + j, block_send.at[CHUNKS + j])

        relay_steps(t)
        each_kind(t - STAGES[0], second_step)
        each_kind(t - STAGES[1], third_step)
        unit = t - STAGES[2]

        @pl.when((unit >= 0) & (unit < units) & jnp.logical_not(pair_first(unit, z_lo)))
        def _():
            last_step(unit)

        return carry

    relay_steps(-1)
    lax.fori_loop(0, ITERATIONS, step, 0)

    def finish(unit, carry):
        store(unit).wait()
        ahead = pair_first(unit, 1 - z_lo)

        @pl.when(ahead)
        def _():
            for toward in range(RING):
                early_copy(early_at(unit, toward, 1 - z_lo)).wait_send()

        @pl.when(jnp.logical_not(ahead))
        def _():
            pair_copy(unit).wait_send()
            for way in range(2):
                first_copy(unit * 2, way).wait_send()
                second_copy(unit * 2, way).wait_send()

        for way in range(2):
            first_copy(unit * 2 + 1, way).wait_send()
            second_copy(unit * 2 + 1, way).wait_send()
        return carry

    lax.fori_loop(0, units, finish, 0)

    def sent(at):
        send(
            block(own, 0), block(partner, 0), block_send.at[at], block_recv.at[0], twin
        ).wait_send()

    for j in range(CHUNKS):
        sent(j)

        @pl.when(seconds)
        def _():
            sent(CHUNKS + j)
            sent(2 * CHUNKS + j)

    for slot in range(units // 4):

        @pl.when((core == 1 - slot // (CHUNKS // 4)) & (y != 0))
        def _():
            sent(3 * CHUNKS + slot)


def on_device(interactions, user_weight):
    users, items = interactions.shape
    slabs = lax.axis_size("slab")
    scale = 1.0 / jnp.sqrt(jnp.float32(users * slabs))
    weights = jnp.stack(
        [jnp.pad(user_weight, (0, PADDED - users)), jnp.full((PADDED,), scale, jnp.float32)]
    )
    width, rows = items // CHUNKS, items // RING
    half = rows // 2
    units = ROUNDS * CHUNKS
    jobs, early = 2 * units, EARLY * RING
    half_type = interactions.dtype
    dma = pltpu.SemaphoreType.DMA
    return pl.pallas_call(
        kernel,
        name="gram_tiles",
        out_shape=jax.ShapeDtypeStruct((ROUNDS, items // slabs, items), jnp.float32),
        in_specs=[
            pl.BlockSpec(memory_space=pl.ANY),
            pl.BlockSpec(memory_space=pltpu.VMEM),
        ],
        out_specs=pl.BlockSpec(memory_space=pl.ANY),
        scratch_shapes=[
            pltpu.VMEM((CHUNKS, PADDED, width), half_type),
            pltpu.VMEM((RING, rows, PADDED), half_type),
            pltpu.VMEM((units, PADDED, width), half_type),
            pltpu.VMEM((units // 4, users, width), half_type),
            pltpu.VMEM((jobs, 2, half // 2, width), half_type),
            pltpu.VMEM((jobs, 2, half // 2, width), half_type),
            pltpu.VMEM((jobs, 2, half, width), half_type),
            pltpu.VMEM((jobs, 2, half, width), half_type),
            pltpu.VMEM((units, half, width), half_type),
            pltpu.VMEM((units, half, width), half_type),
            pltpu.VMEM((early, half, width), half_type),
            pltpu.VMEM((early + 1, half, width), half_type),
            pltpu.VMEM((units, half, width), jnp.float32),
            dma((CHUNKS,)),
            dma((3 * CHUNKS + units // 4,)),
            dma((units,)),
            dma((units // 4,)),
            dma((2, jobs)),
            dma((2, jobs)),
            dma((2, jobs)),
            dma((2, jobs)),
            dma((units,)),
            dma((units,)),
            dma((early,)),
            dma((early,)),
            dma((units,)),
        ],
        compiler_params=pltpu.CompilerParams(
            collective_id=0, has_side_effects=True, vmem_limit_bytes=62 << 20
        ),
        cost_estimate=pl.CostEstimate(
            flops=ROUNDS * 2 * items * items * users,
            bytes_accessed=users * items * 2 + ROUNDS * items // slabs * items * 4,
            transcendentals=0,
        ),
    )(interactions, weights)


def solution(mesh):
    in_specs = (P("slab", "blk"), P("slab"))
    out_specs = P(None, ("blk", "slab"), None)
    return jax.shard_map(
        on_device, mesh=mesh, in_specs=in_specs, out_specs=out_specs, check_vma=False
    )
```

```python
import functools

import jax
import jax.numpy as jnp
import numpy as np
from jax import lax
from jax.experimental import pallas as pl
from jax.experimental.pallas import tpu as pltpu
from jax.sharding import PartitionSpec as P

ROUNDS = 2
CHUNKS = 8
RING = 4
PADDED = 896
PAIR_FIRST = (((), ()), ((5, 7, 9, 11), (4, 6, 8, 10, 12)))
EARLY = max(len(of) for halves in PAIR_FIRST for of in halves)
LAG = 4
STAGES = (1, 3, 5)
ITERATIONS = max([ROUNDS * CHUNKS + STAGES[2]] + [u + LAG + STAGES[1] + 1 for halves in PAIR_FIRST for of in halves for u in of])
PASS_AT = (3, 3, 3, 4, 5, 5, 5, 6)
WRAP_AT = (3, 3, 3, 4, 5, 5, 5, 6)
RELAY_AT = {1: (0, 2, 9, 13), 2: (1, 3, 9, 13), 3: (-1, 1, 7, 11)}
MESH = pl.DeviceIdType.MESH


def kernel(
    x_ref,
    weight_ref,
    out_ref,
    padded_weight,
    own,
    weighted,
    partner,
    relay,
    first_out,
    first_in,
    second_out,
    second_in,
    pair_out,
    pair_in,
    early_out,
    early_in,
    total,
    load_sem,
    block_send,
    block_recv,
    relay_recv,
    first_send,
    first_recv,
    second_send,
    second_recv,
    pair_send,
    pair_recv,
    early_send,
    early_recv,
    store_sem,
):
    blk, slab = lax.axis_index("blk"), lax.axis_index("slab")
    blocks = lax.axis_size("blk")
    core, y = lax.rem(blk, 2), lax.rem(blk // 2, 4)
    x, z_lo = slab // 2, lax.rem(slab, 2)
    users = x_ref.shape[0]
    width = x_ref.shape[1] // CHUNKS
    rows = x_ref.shape[1] // RING
    half = rows // 2
    quarter = half // 2
    scale = np.float32(1) / np.sqrt(np.float32(users * lax.axis_size("slab")))
    units = ROUNDS * CHUNKS
    seconds = core == 1

    right = (blk, lax.rem(x + 1, RING) * 2 + z_lo)
    left = (blk, lax.rem(x + RING - 1, RING) * 2 + z_lo)
    mate = (blk, x * 2 + 1 - z_lo)
    twin = (blk + 1 - 2 * core, slab)
    back = lax.rem(blk + blocks - 2 - core, blocks) + 1
    before = (back, slab)
    front = lax.rem(blk - core + 2, blocks)
    after = ((front, slab), (front + 1, slab))
    base = blk - lax.rem(blk, 8)
    relay_at = [(base + 2 * at + 1 - core, slab) for at in (3, 1, 2)]
    relay_from = (base + 1 - core, slab)
    relay_to = (lax.rem(base + blocks - 8, blocks) + 7, slab)
    relay_after = [(lax.rem(base + 8, blocks) + at, slab) for at in range(2, 8)]

    loads = [
        pltpu.make_async_copy(
            x_ref.at[:, pl.ds(j * width, width)], own.at[j, pl.ds(0, users)], load_sem.at[j]
        )
        for j in range(CHUNKS)
    ]
    for load in loads:
        load.start()

    barrier = pltpu.get_barrier_semaphore()

    def greet(device):
        pl.semaphore_signal(barrier, inc=1, device_id=device, device_id_type=MESH)

    for device in (right, left, mate, twin):
        greet(device)

    @pl.when(seconds)
    def _():
        greet(after[0])
        greet(after[1])

    @pl.when(y != 0)
    def _():
        greet(relay_from)

    @pl.when(seconds & (y == 3))
    def _():
        for device in relay_after:
            greet(device)

    padded_weight[...] = jnp.zeros(padded_weight.shape, padded_weight.dtype)
    padded_weight[:, pl.ds(0, users)] = weight_ref[...]
    own[:, pl.ds(users, PADDED - users), :] = jnp.zeros(
        (CHUNKS, PADDED - users, width), own.dtype
    )
    early_in[early_in.shape[0] - 1] = jnp.zeros((half, width), early_in.dtype)
    partner[:, pl.ds(users, PADDED - users), :] = jnp.zeros(
        (units, PADDED - users, width), partner.dtype
    )
    relays = jnp.where(y == 0, 3, 1)
    pl.semaphore_wait(barrier, 5 + relays)

    def send(source, target, sent, landed, device):
        return pltpu.make_async_remote_copy(
            src_ref=source,
            dst_ref=target,
            send_sem=sent,
            recv_sem=landed,
            device_id=device,
            device_id_type=MESH,
        )

    def block(ref, at):
        return ref.at[at, pl.ds(0, users)]

    def pass_on(j, unit, sent):
        def direct():
            send(block(own, j), block(partner, unit), sent, block_recv.at[unit], before).start()

        if j % 4 == 0:
            direct()
        else:
            slot = unit // 4

            @pl.when(y == 0)
            def _():
                send(
                    block(own, j), relay.at[slot], sent, relay_recv.at[slot], relay_at[j % 4 - 1]
                ).start()

            @pl.when(y != 0)
            def _():
                direct()

    def relay_on(slot):
        unit = slot * 4 + lax.rem(y, 3) + 1
        sent = block_send.at[3 * CHUNKS + slot]
        send(relay.at[slot], relay.at[slot], sent, relay_recv.at[slot], relay_to).wait_recv()
        send(relay.at[slot], block(partner, unit), sent, block_recv.at[unit], relay_to).start()

    for j in range(CHUNKS):
        loads[j].wait()

        @pl.when(core == 0)
        def _():
            pass_on(j, j, block_send.at[j])

        @pl.when(seconds)
        def _():
            send(
                block(own, j), block(partner, j), block_send.at[j], block_recv.at[j], twin
            ).start()

    def weigh(step):
        for piece in range(rows // width):
            values = own[lax.rem(x + step, RING) * (rows // width) + piece].T.astype(jnp.float32)
            weighted[step, pl.ds(piece * width, width)] = (
                values * padded_weight[...] * scale
            ).astype(weighted.dtype)

    def weigh_rest():
        for step in (1, 3, 0):
            weigh(step)

    def gram(step, unit, part):
        start = pl.multiple_of(part * half, half)
        return jnp.dot(
            weighted[step, pl.ds(start, half)],
            partner[unit],
            preferred_element_type=jnp.float32,
        )

    weigh(2)

    @pl.when(seconds)
    def _():
        weigh_rest()

    def pair_first(unit, part):
        def among(of):
            return functools.reduce(jnp.logical_or, [unit == u for u in of], unit < 0)

        at = [[among(of) for of in halves] for halves in PAIR_FIRST]
        return jnp.where(
            core == 0,
            jnp.where(part == 0, at[0][0], at[0][1]),
            jnp.where(part == 0, at[1][0], at[1][1]),
        )

    def relay_steps(t):
        for slot in range(units // 4):
            at = jnp.where(y == 1, RELAY_AT[1][slot], jnp.where(y == 2, RELAY_AT[2][slot], RELAY_AT[3][slot]))

            @pl.when((core == 1 - slot // (CHUNKS // 4)) & (y != 0) & (t == at))
            def _():
                relay_on(slot)

    def first_copy(job, way):
        return send(
            first_out.at[job, way],
            first_in.at[job, way],
            first_send.at[way, job],
            first_recv.at[way, job],
            (right, left)[way],
        )

    def second_copy(job, way):
        return send(
            second_out.at[job, way],
            second_in.at[job, way],
            second_send.at[way, job],
            second_recv.at[way, job],
            (right, left)[way],
        )

    def pair_copy(unit):
        return send(
            pair_out.at[unit], pair_in.at[unit], pair_send.at[unit], pair_recv.at[unit], mate
        )

    def early_copy(at):
        return send(
            early_out.at[at], early_in.at[at], early_send.at[at], early_recv.at[at], mate
        )

    def early_at(unit, step, part):
        before = [[sum([jnp.where(unit > u, 1, 0) for u in of]) for of in halves] for halves in PAIR_FIRST]
        at = jnp.where(
            core == 0,
            jnp.where(part == 0, before[0][0], before[0][1]),
            jnp.where(part == 0, before[1][0], before[1][1]),
        )
        return at * RING + step

    def store(unit):
        column = pl.multiple_of(lax.rem(unit, CHUNKS) * width, width)
        return pltpu.make_async_copy(
            pair_in.at[unit],
            out_ref.at[unit // CHUNKS, :, pl.ds(column, width)],
            store_sem.at[unit],
        )

    def forward(unit):
        return send(
            block(partner, unit),
            block(partner, unit + CHUNKS),
            block_send.at[2 * CHUNKS + unit],
            block_recv.at[unit + CHUNKS],
            twin,
        )

    def job_of(kind, stage):
        late = kind == 2
        unit = stage - jnp.where(late, LAG, 0)
        mine = jnp.where(kind > 0, 1, 0)
        part = jnp.where(kind > 0, z_lo, 1 - z_lo)
        active = (unit >= 0) & (unit < units) & (pair_first(unit, part) == late)
        return late, unit, mine, part, active

    def each_kind(stage, work):
        def one(kind, carry):
            late, unit, mine, part, active = job_of(kind, stage)

            @pl.when(active)
            def _():
                work(late, unit, mine, part, unit * 2 + mine)

            return carry

        lax.fori_loop(0, 3, one, 0)

    def paired(late, unit, step, part):
        at = jnp.where(late, early_at(unit, step, part), early_in.shape[0] - 1)

        @pl.when(late)
        def _():
            early_copy(at).wait_recv()

        return gram(step, unit, part) + early_in[at].astype(jnp.float32)

    def first_step(late, unit, mine, part, job):
        value = paired(late, unit, 2, part).astype(first_out.dtype)
        for way in range(2):
            first_out[job, way] = value[way * quarter : (way + 1) * quarter]
            first_copy(job, way).start()

    def second_step(late, unit, mine, part, job):
        for way in range(2):
            value = paired(late, unit, (1, 3)[way], part)
            first_copy(job, way).wait_recv()
            joined = slice(way * quarter, (way + 1) * quarter)
            plain = slice((1 - way) * quarter, (2 - way) * quarter)
            second_out[job, way, joined] = (
                value[joined] + first_in[job, way].astype(jnp.float32)
            ).astype(second_out.dtype)
            second_out[job, way, plain] = value[plain].astype(second_out.dtype)
            second_copy(job, way).start()

    def third_step(late, unit, mine, part, job):
        value = paired(late, unit, 0, part)
        for way in range(2):
            second_copy(job, way).wait_recv()
        value = (
            value
            + second_in[job, 0].astype(jnp.float32)
            + second_in[job, 1].astype(jnp.float32)
        )

        @pl.when(mine == 0)
        def _():
            pair_out[unit] = value.astype(pair_out.dtype)
            pair_copy(unit).start()

        @pl.when((mine == 1) & jnp.logical_not(late))
        def _():
            total[unit] = value

        @pl.when(late)
        def _():
            pair_in[unit] = value.astype(pair_in.dtype)
            store(unit).start()

    def last_step(unit):
        pair_copy(unit).wait_recv()
        pair_in[unit] = (total[unit] + pair_in[unit].astype(jnp.float32)).astype(pair_in.dtype)
        store(unit).start()

    def step(t, carry):
        @pl.when(t < units)
        def _():
            send(
                block(partner, t), block(partner, t), block_send.at[0], block_recv.at[t], twin
            ).wait_recv()

            @pl.when(seconds & (t < CHUNKS))
            def _():
                forward(t).start()

            @pl.when(pair_first(t, 1 - z_lo))
            def _():
                def early(i, carry):
                    toward = lax.rem(i + 2, RING)
                    at = early_at(t, toward, 1 - z_lo)
                    early_out[at] = gram(toward, t, 1 - z_lo).astype(early_out.dtype)
                    early_copy(at).start()
                    return carry

                lax.fori_loop(0, RING, early, 0)

        each_kind(t, first_step)

        @pl.when((core == 0) & (t == 0))
        def _():
            weigh_rest()

        for j in range(CHUNKS):

            @pl.when(seconds & (t == jnp.where(y == 0, WRAP_AT[j], PASS_AT[j])))
            def _():
                pass_on(j, CHUNKS + j, block_send.at[CHUNKS + j])

        relay_steps(t)
        each_kind(t - STAGES[0], second_step)
        each_kind(t - STAGES[1], third_step)
        unit = t - STAGES[2]

        @pl.when((unit >= 0) & (unit < units) & jnp.logical_not(pair_first(unit, z_lo)))
        def _():
            last_step(unit)

        return carry

    relay_steps(-1)
    lax.fori_loop(0, ITERATIONS, step, 0)

    def finish(unit, carry):
        store(unit).wait()
        ahead = pair_first(unit, 1 - z_lo)

        @pl.when(ahead)
        def _():
            for toward in range(RING):
                early_copy(early_at(unit, toward, 1 - z_lo)).wait_send()

        @pl.when(jnp.logical_not(ahead))
        def _():
            pair_copy(unit).wait_send()
            for way in range(2):
                first_copy(unit * 2, way).wait_send()
                second_copy(unit * 2, way).wait_send()

        for way in range(2):
            first_copy(unit * 2 + 1, way).wait_send()
            second_copy(unit * 2 + 1, way).wait_send()
        return carry

    lax.fori_loop(0, units, finish, 0)

    def sent(at):
        send(
            block(own, 0), block(partner, 0), block_send.at[at], block_recv.at[0], twin
        ).wait_send()

    for j in range(CHUNKS):
        sent(j)

        @pl.when(seconds)
        def _():
            sent(CHUNKS + j)
            sent(2 * CHUNKS + j)

    for slot in range(units // 4):

        @pl.when((core == 1 - slot // (CHUNKS // 4)) & (y != 0))
        def _():
            sent(3 * CHUNKS + slot)


def on_device(interactions, user_weight):
    users, items = interactions.shape
    slabs = lax.axis_size("slab")
    width, rows = items // CHUNKS, items // RING
    half = rows // 2
    units = ROUNDS * CHUNKS
    jobs, early = 2 * units, EARLY * RING
    half_type = interactions.dtype
    dma = pltpu.SemaphoreType.DMA
    tiles = pl.pallas_call(
        kernel,
        name="gram_tiles",
        out_shape=jax.ShapeDtypeStruct((ROUNDS, items // slabs, items), half_type),
        in_specs=[
            pl.BlockSpec(memory_space=pl.ANY),
            pl.BlockSpec(memory_space=pltpu.VMEM),
        ],
        out_specs=pl.BlockSpec(memory_space=pl.ANY),
        scratch_shapes=[
            pltpu.VMEM((1, PADDED), jnp.float32),
            pltpu.VMEM((CHUNKS, PADDED, width), half_type),
            pltpu.VMEM((RING, rows, PADDED), half_type),
            pltpu.VMEM((units, PADDED, width), half_type),
            pltpu.VMEM((units // 4, users, width), half_type),
            pltpu.VMEM((jobs, 2, half // 2, width), half_type),
            pltpu.VMEM((jobs, 2, half // 2, width), half_type),
            pltpu.VMEM((jobs, 2, half, width), half_type),
            pltpu.VMEM((jobs, 2, half, width), half_type),
            pltpu.VMEM((units, half, width), half_type),
            pltpu.VMEM((units, half, width), half_type),
            pltpu.VMEM((early, half, width), half_type),
            pltpu.VMEM((early + 1, half, width), half_type),
            pltpu.VMEM((units, half, width), jnp.float32),
            dma((CHUNKS,)),
            dma((3 * CHUNKS + units // 4,)),
            dma((units,)),
            dma((units // 4,)),
            dma((2, jobs)),
            dma((2, jobs)),
            dma((2, jobs)),
            dma((2, jobs)),
            dma((units,)),
            dma((units,)),
            dma((early,)),
            dma((early,)),
            dma((units,)),
        ],
        compiler_params=pltpu.CompilerParams(
            collective_id=0, has_side_effects=True, vmem_limit_bytes=62 << 20
        ),
        cost_estimate=pl.CostEstimate(
            flops=ROUNDS * 2 * items * items * users,
            bytes_accessed=users * items * 2 + ROUNDS * items // slabs * items * 2,
            transcendentals=0,
        ),
    )(interactions, user_weight.reshape(1, users))
    return tiles.astype(jnp.float32)


def solution(mesh):
    in_specs = (P("slab", "blk"), P("slab"))
    out_specs = P(None, ("blk", "slab"), None)
    return jax.shard_map(
        on_device, mesh=mesh, in_specs=in_specs, out_specs=out_specs, check_vma=False
    )
```

```python
import functools

import jax
import jax.numpy as jnp
import numpy as np
from jax import lax
from jax.experimental import pallas as pl
from jax.experimental.pallas import tpu as pltpu
from jax.sharding import PartitionSpec as P

ROUNDS = 2
CHUNKS = 8
RING = 4
PADDED = 896
PAIR_FIRST = ((((10, 12), (10, 12)), ((5, 7, 9, 11), (4, 6, 8, 10, 12))), (((), ()), ((5, 7, 9, 11), (4, 6, 8, 10, 12))))
EARLY = max(len(of) for cores in PAIR_FIRST for halves in cores for of in halves)
LAG = 6
STAGES = (1, 3, 8)
ITERATIONS = max([ROUNDS * CHUNKS + STAGES[2]] + [u + LAG + STAGES[1] + 1 for cores in PAIR_FIRST for halves in cores for of in halves for u in of])
PASS_AT = (3, 3, 3, 4, 5, 5, 5, 6)
WRAP_AT = (3, 2, 2, 3, 4, 3, 4, 4)
RELAY_AT = {1: (1, 3, 7, 10), 2: (0, 2, 8, 11), 3: (-1, 1, 6, 9)}
AGAIN_AT = (3, 5, 9, 12)
MESH = pl.DeviceIdType.MESH


def kernel(
    x_ref,
    weight_ref,
    out_ref,
    padded_weight,
    own,
    weighted,
    partner,
    relay,
    relay2,
    first_out,
    first_in,
    second_out,
    second_in,
    pair_out,
    pair_in,
    early_out,
    early_in,
    total,
    load_sem,
    block_send,
    block_recv,
    relay_recv,
    relay2_recv,
    first_send,
    first_recv,
    second_send,
    second_recv,
    pair_send,
    pair_recv,
    early_send,
    early_recv,
    store_sem,
):
    blk, slab = lax.axis_index("blk"), lax.axis_index("slab")
    blocks = lax.axis_size("blk")
    core, y = lax.rem(blk, 2), lax.rem(blk // 2, 4)
    x, z_lo = slab // 2, lax.rem(slab, 2)
    users = x_ref.shape[0]
    width = x_ref.shape[1] // CHUNKS
    rows = x_ref.shape[1] // RING
    half = rows // 2
    quarter = half // 2
    scale = np.float32(1) / np.sqrt(np.float32(users * lax.axis_size("slab")))
    units = ROUNDS * CHUNKS
    seconds = core == 1

    right = (blk, lax.rem(x + 1, RING) * 2 + z_lo)
    left = (blk, lax.rem(x + RING - 1, RING) * 2 + z_lo)
    mate = (blk, x * 2 + 1 - z_lo)
    twin = (blk + 1 - 2 * core, slab)
    back = lax.rem(blk + blocks - 2 - core, blocks) + 1
    before = (back, slab)
    front = lax.rem(blk - core + 2, blocks)
    after = ((front, slab), (front + 1, slab))
    base = blk - lax.rem(blk, 8)
    relay_at = [(base + 2 * at + 1 - core, slab) for at in (3, 2, 1)]
    relay_from = (base + 1 - core, slab)
    onward = lax.rem(base + blocks - 8, blocks)
    relay_to = (onward + jnp.where(y == 1, 4 + core, 7), slab)
    second_to = (base + 7, slab)
    second_from = (lax.rem(base + 8, blocks) + 2 + core, slab)
    relay_after = [(lax.rem(base + 8, blocks) + at, slab) for at in range(4, 8)]

    loads = [
        pltpu.make_async_copy(
            x_ref.at[:, pl.ds(j * width, width)], own.at[j, pl.ds(0, users)], load_sem.at[j]
        )
        for j in range(CHUNKS)
    ]
    for load in loads:
        load.start()

    barrier = pltpu.get_barrier_semaphore()

    def greet(device):
        pl.semaphore_signal(barrier, inc=1, device_id=device, device_id_type=MESH)

    for device in (right, left, mate, twin):
        greet(device)

    @pl.when(seconds)
    def _():
        greet(after[0])
        greet(after[1])

    @pl.when(y != 0)
    def _():
        greet(relay_from)

    @pl.when(seconds & (y == 3))
    def _():
        for device in relay_after:
            greet(device)
        greet((base + 4, slab))
        greet((base + 5, slab))

    @pl.when(y == 2)
    def _():
        greet(second_from)

    padded_weight[...] = jnp.zeros(padded_weight.shape, padded_weight.dtype)
    padded_weight[:, pl.ds(0, users)] = weight_ref[...]
    own[:, pl.ds(users, PADDED - users), :] = jnp.zeros(
        (CHUNKS, PADDED - users, width), own.dtype
    )
    early_in[early_in.shape[0] - 1] = jnp.zeros((half, width), early_in.dtype)
    partner[:, pl.ds(users, PADDED - users), :] = jnp.zeros(
        (units, PADDED - users, width), partner.dtype
    )
    relays = jnp.where(y == 0, 3, jnp.where(y == 2, 2, 1))
    pl.semaphore_wait(barrier, 5 + relays)

    def send(source, target, sent, landed, device):
        return pltpu.make_async_remote_copy(
            src_ref=source,
            dst_ref=target,
            send_sem=sent,
            recv_sem=landed,
            device_id=device,
            device_id_type=MESH,
        )

    def block(ref, at):
        return ref.at[at, pl.ds(0, users)]

    def pass_on(j, unit, sent):
        def direct():
            send(block(own, j), block(partner, unit), sent, block_recv.at[unit], before).start()

        if j % 4 == 0:
            direct()
        else:
            slot = unit // 4

            @pl.when(y == 0)
            def _():
                send(
                    block(own, j), relay.at[slot], sent, relay_recv.at[slot], relay_at[j % 4 - 1]
                ).start()

            @pl.when(y != 0)
            def _():
                direct()

    def relay_on(slot):
        sent = block_send.at[3 * CHUNKS + slot]
        send(relay.at[slot], relay.at[slot], sent, relay_recv.at[slot], relay_to).wait_recv()

        @pl.when(y == 1)
        def _():
            send(
                relay.at[slot], relay2.at[slot], sent, relay2_recv.at[slot], relay_to
            ).start()

        @pl.when(y != 1)
        def _():
            unit = slot * 4 + 4 - y
            send(
                relay.at[slot], block(partner, unit), sent, block_recv.at[unit], relay_to
            ).start()

    def relay_again(slot):
        unit = slot * 4 + 3
        sent = block_send.at[3 * CHUNKS + units // 4 + slot]
        send(
            relay2.at[slot], relay2.at[slot], sent, relay2_recv.at[slot], second_to
        ).wait_recv()
        send(
            relay2.at[slot], block(partner, unit), sent, block_recv.at[unit], second_to
        ).start()

    for j in range(CHUNKS):
        loads[j].wait()

        @pl.when(core == 0)
        def _():
            pass_on(j, j, block_send.at[j])

        @pl.when(seconds)
        def _():
            send(
                block(own, j), block(partner, j), block_send.at[j], block_recv.at[j], twin
            ).start()

    def weigh(step):
        for piece in range(rows // width):
            values = own[lax.rem(x + step, RING) * (rows // width) + piece].T.astype(jnp.float32)
            weighted[step, pl.ds(piece * width, width)] = (
                values * padded_weight[...] * scale
            ).astype(weighted.dtype)

    def weigh_rest():
        for step in (1, 3, 0):
            weigh(step)

    def gram(step, unit, part):
        start = pl.multiple_of(part * half, half)
        return jnp.dot(
            weighted[step, pl.ds(start, half)],
            partner[unit],
            preferred_element_type=jnp.float32,
        )

    weigh(2)

    @pl.when(seconds)
    def _():
        weigh_rest()

    def of_this(values):
        def pick(part):
            return jnp.where(
                y == 3,
                jnp.where(core == 0, values[1][0][part], values[1][1][part]),
                jnp.where(core == 0, values[0][0][part], values[0][1][part]),
            )

        return lambda part: jnp.where(part == 0, pick(0), pick(1))

    def tabulate(work):
        return [[[work(of) for of in halves] for halves in cores] for cores in PAIR_FIRST]

    def pair_first(unit, part):
        def among(of):
            return sum([jnp.where(unit == u, 1, 0) for u in of], 0 * unit)

        return of_this(tabulate(among))(part) == 1

    def relay_steps(t):
        for slot in range(units // 4):
            at = jnp.where(y == 1, RELAY_AT[1][slot], jnp.where(y == 2, RELAY_AT[2][slot], RELAY_AT[3][slot]))

            @pl.when((core == 1 - slot // (CHUNKS // 4)) & (y != 0) & (t == at))
            def _():
                relay_on(slot)

            @pl.when((core == 1 - slot // (CHUNKS // 4)) & (y == 2) & (t == AGAIN_AT[slot]))
            def _():
                relay_again(slot)

    def first_copy(job, way):
        return send(
            first_out.at[job, way],
            first_in.at[job, way],
            first_send.at[way, job],
            first_recv.at[way, job],
            (right, left)[way],
        )

    def second_copy(job, way):
        return send(
            second_out.at[job, way],
            second_in.at[job, way],
            second_send.at[way, job],
            second_recv.at[way, job],
            (right, left)[way],
        )

    def pair_copy(unit):
        return send(
            pair_out.at[unit], pair_in.at[unit], pair_send.at[unit], pair_recv.at[unit], mate
        )

    def early_copy(at):
        return send(
            early_out.at[at], early_in.at[at], early_send.at[at], early_recv.at[at], mate
        )

    def early_at(unit, step, part):
        def rank(of):
            return sum([jnp.where(unit > u, 1, 0) for u in of], 0 * unit)

        return of_this(tabulate(rank))(part) * RING + step

    def store(unit):
        column = pl.multiple_of(lax.rem(unit, CHUNKS) * width, width)
        return pltpu.make_async_copy(
            pair_in.at[unit],
            out_ref.at[unit // CHUNKS, :, pl.ds(column, width)],
            store_sem.at[unit],
        )

    def forward(unit):
        return send(
            block(partner, unit),
            block(partner, unit + CHUNKS),
            block_send.at[2 * CHUNKS + unit],
            block_recv.at[unit + CHUNKS],
            twin,
        )

    def job_of(kind, stage):
        late = kind == 2
        unit = stage - jnp.where(late, LAG, 0)
        mine = jnp.where(kind > 0, 1, 0)
        part = jnp.where(kind > 0, z_lo, 1 - z_lo)
        active = (unit >= 0) & (unit < units) & (pair_first(unit, part) == late)
        return late, unit, mine, part, active

    def each_kind(stage, work):
        def one(kind, carry):
            late, unit, mine, part, active = job_of(kind, stage)

            @pl.when(active)
            def _():
                work(late, unit, mine, part, unit * 2 + mine)

            return carry

        lax.fori_loop(0, 3, one, 0)

    def paired(late, unit, step, part):
        at = jnp.where(late, early_at(unit, step, part), early_in.shape[0] - 1)

        @pl.when(late)
        def _():
            early_copy(at).wait_recv()

        return gram(step, unit, part) + early_in[at].astype(jnp.float32)

    def first_step(late, unit, mine, part, job):
        value = paired(late, unit, 2, part).astype(first_out.dtype)
        for way in range(2):
            first_out[job, way] = value[way * quarter : (way + 1) * quarter]
            first_copy(job, way).start()

    def second_step(late, unit, mine, part, job):
        for way in range(2):
            value = paired(late, unit, (1, 3)[way], part)
            first_copy(job, way).wait_recv()
            joined = slice(way * quarter, (way + 1) * quarter)
            plain = slice((1 - way) * quarter, (2 - way) * quarter)
            second_out[job, way, joined] = (
                value[joined] + first_in[job, way].astype(jnp.float32)
            ).astype(second_out.dtype)
            second_out[job, way, plain] = value[plain].astype(second_out.dtype)
            second_copy(job, way).start()

    def third_step(late, unit, mine, part, job):
        value = paired(late, unit, 0, part)
        for way in range(2):
            second_copy(job, way).wait_recv()
        value = (
            value
            + second_in[job, 0].astype(jnp.float32)
            + second_in[job, 1].astype(jnp.float32)
        )

        @pl.when(mine == 0)
        def _():
            pair_out[unit] = value.astype(pair_out.dtype)
            pair_copy(unit).start()

        @pl.when((mine == 1) & jnp.logical_not(late))
        def _():
            total[unit] = value

        @pl.when(late)
        def _():
            pair_in[unit] = value.astype(pair_in.dtype)
            store(unit).start()

    def last_step(unit):
        pair_copy(unit).wait_recv()
        pair_in[unit] = (total[unit] + pair_in[unit].astype(jnp.float32)).astype(pair_in.dtype)
        store(unit).start()

    def step(t, carry):
        @pl.when(t < units)
        def _():
            send(
                block(partner, t), block(partner, t), block_send.at[0], block_recv.at[t], twin
            ).wait_recv()

            @pl.when(seconds & (t < CHUNKS))
            def _():
                forward(t).start()

            @pl.when(pair_first(t, 1 - z_lo))
            def _():
                def early(i, carry):
                    toward = lax.rem(i + 2, RING)
                    at = early_at(t, toward, 1 - z_lo)
                    early_out[at] = gram(toward, t, 1 - z_lo).astype(early_out.dtype)
                    early_copy(at).start()
                    return carry

                lax.fori_loop(0, RING, early, 0)

        each_kind(t, first_step)

        @pl.when((core == 0) & (t == 0))
        def _():
            weigh_rest()

        for j in range(CHUNKS):

            @pl.when(seconds & (t == jnp.where(y == 0, WRAP_AT[j], PASS_AT[j])))
            def _():
                pass_on(j, CHUNKS + j, block_send.at[CHUNKS + j])

        relay_steps(t)
        each_kind(t - STAGES[0], second_step)
        each_kind(t - STAGES[1], third_step)
        unit = t - STAGES[2]

        @pl.when((unit >= 0) & (unit < units) & jnp.logical_not(pair_first(unit, z_lo)))
        def _():
            last_step(unit)

        return carry

    relay_steps(-1)
    lax.fori_loop(0, ITERATIONS, step, 0)

    def finish(unit, carry):
        store(unit).wait()
        ahead = pair_first(unit, 1 - z_lo)

        @pl.when(ahead)
        def _():
            for toward in range(RING):
                early_copy(early_at(unit, toward, 1 - z_lo)).wait_send()

        @pl.when(jnp.logical_not(ahead))
        def _():
            pair_copy(unit).wait_send()
            for way in range(2):
                first_copy(unit * 2, way).wait_send()
                second_copy(unit * 2, way).wait_send()

        for way in range(2):
            first_copy(unit * 2 + 1, way).wait_send()
            second_copy(unit * 2 + 1, way).wait_send()
        return carry

    lax.fori_loop(0, units, finish, 0)

    def sent(at):
        send(
            block(own, 0), block(partner, 0), block_send.at[at], block_recv.at[0], twin
        ).wait_send()

    for j in range(CHUNKS):
        sent(j)

        @pl.when(seconds)
        def _():
            sent(CHUNKS + j)
            sent(2 * CHUNKS + j)

    for slot in range(units // 4):

        @pl.when((core == 1 - slot // (CHUNKS // 4)) & (y != 0))
        def _():
            sent(3 * CHUNKS + slot)

        @pl.when((core == 1 - slot // (CHUNKS // 4)) & (y == 2))
        def _():
            sent(3 * CHUNKS + units // 4 + slot)


def on_device(interactions, user_weight):
    users, items = interactions.shape
    slabs = lax.axis_size("slab")
    width, rows = items // CHUNKS, items // RING
    half = rows // 2
    units = ROUNDS * CHUNKS
    jobs, early = 2 * units, EARLY * RING
    half_type = interactions.dtype
    dma = pltpu.SemaphoreType.DMA
    tiles = pl.pallas_call(
        kernel,
        name="gram_tiles",
        out_shape=jax.ShapeDtypeStruct((ROUNDS, items // slabs, items), half_type),
        in_specs=[
            pl.BlockSpec(memory_space=pl.ANY),
            pl.BlockSpec(memory_space=pltpu.VMEM),
        ],
        out_specs=pl.BlockSpec(memory_space=pl.ANY),
        scratch_shapes=[
            pltpu.VMEM((1, PADDED), jnp.float32),
            pltpu.VMEM((CHUNKS, PADDED, width), half_type),
            pltpu.VMEM((RING, rows, PADDED), half_type),
            pltpu.VMEM((units, PADDED, width), half_type),
            pltpu.VMEM((units // 4, users, width), half_type),
            pltpu.VMEM((units // 4, users, width), half_type),
            pltpu.VMEM((jobs, 2, half // 2, width), half_type),
            pltpu.VMEM((jobs, 2, half // 2, width), half_type),
            pltpu.VMEM((jobs, 2, half, width), half_type),
            pltpu.VMEM((jobs, 2, half, width), half_type),
            pltpu.VMEM((units, half, width), half_type),
            pltpu.VMEM((units, half, width), half_type),
            pltpu.VMEM((early, half, width), half_type),
            pltpu.VMEM((early + 1, half, width), half_type),
            pltpu.VMEM((units, half, width), jnp.float32),
            dma((CHUNKS,)),
            dma((3 * CHUNKS + units // 2,)),
            dma((units,)),
            dma((units // 4,)),
            dma((units // 4,)),
            dma((2, jobs)),
            dma((2, jobs)),
            dma((2, jobs)),
            dma((2, jobs)),
            dma((units,)),
            dma((units,)),
            dma((early,)),
            dma((early,)),
            dma((units,)),
        ],
        compiler_params=pltpu.CompilerParams(
            collective_id=0, has_side_effects=True, vmem_limit_bytes=62 << 20
        ),
        cost_estimate=pl.CostEstimate(
            flops=ROUNDS * 2 * items * items * users,
            bytes_accessed=users * items * 2 + ROUNDS * items // slabs * items * 2,
            transcendentals=0,
        ),
    )(interactions, user_weight.reshape(1, users))
    return tiles.astype(jnp.float32)


def solution(mesh):
    in_specs = (P("slab", "blk"), P("slab"))
    out_specs = P(None, ("blk", "slab"), None)
    return jax.shard_map(
        on_device, mesh=mesh, in_specs=in_specs, out_specs=out_specs, check_vma=False
    )
```

```python
import functools

import jax
import jax.numpy as jnp
import numpy as np
from jax import lax
from jax.experimental import pallas as pl
from jax.experimental.pallas import tpu as pltpu
from jax.sharding import PartitionSpec as P

ROUNDS = 2
CHUNKS = 8
RING = 4
PADDED = 896
PAIR_FIRST = ((((10, 12), (10, 12)), ((5, 7, 9, 11), (4, 6, 8, 10, 12))), (((), ()), ((5, 7, 9, 11), (4, 6, 8, 10, 12))))
EARLY = max(len(of) for cores in PAIR_FIRST for halves in cores for of in halves)
LAG = 6
STAGES = (1, 3, 8)
ITERATIONS = max([ROUNDS * CHUNKS + STAGES[2]] + [u + LAG + STAGES[1] + 1 for cores in PAIR_FIRST for halves in cores for of in halves for u in of])
PASS_AT = (2, 2, 3, 3, 4, 4, 5, 5)
WRAP_AT = (3, 2, 2, 2, 3, 3, 3, 3)
RELAY_AT = {1: (1, 3, 6, 9), 2: (0, 2, 7, 10), 3: (-1, 1, 6, 8)}
AGAIN_AT = (3, 5, 8, 11)
MESH = pl.DeviceIdType.MESH


def kernel(
    x_ref,
    weight_ref,
    out_ref,
    padded_weight,
    own,
    weighted,
    partner,
    relay,
    relay2,
    first_out,
    first_in,
    second_out,
    second_in,
    pair_out,
    pair_in,
    early_out,
    early_in,
    total,
    load_sem,
    block_send,
    block_recv,
    relay_recv,
    relay2_recv,
    first_send,
    first_recv,
    second_send,
    second_recv,
    pair_send,
    pair_recv,
    early_send,
    early_recv,
    store_sem,
):
    blk, slab = lax.axis_index("blk"), lax.axis_index("slab")
    blocks = lax.axis_size("blk")
    core, y = lax.rem(blk, 2), lax.rem(blk // 2, 4)
    x, z_lo = slab // 2, lax.rem(slab, 2)
    users = x_ref.shape[0]
    width = x_ref.shape[1] // CHUNKS
    rows = x_ref.shape[1] // RING
    half = rows // 2
    quarter = half // 2
    scale = np.float32(1) / np.sqrt(np.float32(users * lax.axis_size("slab")))
    units = ROUNDS * CHUNKS
    seconds = core == 1

    right = (blk, lax.rem(x + 1, RING) * 2 + z_lo)
    left = (blk, lax.rem(x + RING - 1, RING) * 2 + z_lo)
    mate = (blk, x * 2 + 1 - z_lo)
    twin = (blk + 1 - 2 * core, slab)
    back = lax.rem(blk + blocks - 2 - core, blocks) + 1
    before = (back, slab)
    front = lax.rem(blk - core + 2, blocks)
    after = ((front, slab), (front + 1, slab))
    base = blk - lax.rem(blk, 8)
    relay_at = [(base + 2 * at + 1 - core, slab) for at in (3, 2, 1)]
    relay_from = (base + 1 - core, slab)
    onward = lax.rem(base + blocks - 8, blocks)
    relay_to = (onward + jnp.where(y == 1, 4 + core, 7), slab)
    second_to = (base + 7, slab)
    second_from = (lax.rem(base + 8, blocks) + 2 + core, slab)
    relay_after = [(lax.rem(base + 8, blocks) + at, slab) for at in range(4, 8)]

    loads = [
        pltpu.make_async_copy(
            x_ref.at[:, pl.ds(j * width, width)], own.at[j, pl.ds(0, users)], load_sem.at[j]
        )
        for j in range(CHUNKS)
    ]
    for load in loads:
        load.start()

    barrier = pltpu.get_barrier_semaphore()

    def greet(device):
        pl.semaphore_signal(barrier, inc=1, device_id=device, device_id_type=MESH)

    for device in (right, left, mate, twin):
        greet(device)

    @pl.when(seconds)
    def _():
        greet(after[0])
        greet(after[1])

    @pl.when(y != 0)
    def _():
        greet(relay_from)

    @pl.when(seconds & (y == 3))
    def _():
        for device in relay_after:
            greet(device)
        greet((base + 4, slab))
        greet((base + 5, slab))

    @pl.when(y == 2)
    def _():
        greet(second_from)

    padded_weight[...] = jnp.zeros(padded_weight.shape, padded_weight.dtype)
    padded_weight[:, pl.ds(0, users)] = weight_ref[...]
    own[:, pl.ds(users, PADDED - users), :] = jnp.zeros(
        (CHUNKS, PADDED - users, width), own.dtype
    )
    early_in[early_in.shape[0] - 1] = jnp.zeros((half, width), early_in.dtype)
    partner[:, pl.ds(users, PADDED - users), :] = jnp.zeros(
        (units, PADDED - users, width), partner.dtype
    )
    relays = jnp.where(y == 0, 3, jnp.where(y == 2, 2, 1))
    pl.semaphore_wait(barrier, 5 + relays)

    def send(source, target, sent, landed, device):
        return pltpu.make_async_remote_copy(
            src_ref=source,
            dst_ref=target,
            send_sem=sent,
            recv_sem=landed,
            device_id=device,
            device_id_type=MESH,
        )

    def block(ref, at):
        return ref.at[at, pl.ds(0, users)]

    def pass_on(j, unit, sent):
        def direct():
            send(block(own, j), block(partner, unit), sent, block_recv.at[unit], before).start()

        if j % 4 == 0:
            direct()
        else:
            slot = unit // 4

            @pl.when(y == 0)
            def _():
                send(
                    block(own, j), relay.at[slot], sent, relay_recv.at[slot], relay_at[j % 4 - 1]
                ).start()

            @pl.when(y != 0)
            def _():
                direct()

    def relay_on(slot):
        sent = block_send.at[3 * CHUNKS + slot]
        send(relay.at[slot], relay.at[slot], sent, relay_recv.at[slot], relay_to).wait_recv()

        @pl.when(y == 1)
        def _():
            send(
                relay.at[slot], relay2.at[slot], sent, relay2_recv.at[slot], relay_to
            ).start()

        @pl.when(y != 1)
        def _():
            unit = slot * 4 + 4 - y
            send(
                relay.at[slot], block(partner, unit), sent, block_recv.at[unit], relay_to
            ).start()

    def relay_again(slot):
        unit = slot * 4 + 3
        sent = block_send.at[3 * CHUNKS + units // 4 + slot]
        send(
            relay2.at[slot], relay2.at[slot], sent, relay2_recv.at[slot], second_to
        ).wait_recv()
        send(
            relay2.at[slot], block(partner, unit), sent, block_recv.at[unit], second_to
        ).start()

    for j in range(CHUNKS):
        loads[j].wait()

        @pl.when(core == 0)
        def _():
            pass_on(j, j, block_send.at[j])

        @pl.when(seconds)
        def _():
            send(
                block(own, j), block(partner, j), block_send.at[j], block_recv.at[j], twin
            ).start()

    def weigh(step):
        for piece in range(rows // width):
            values = own[lax.rem(x + step, RING) * (rows // width) + piece].T.astype(jnp.float32)
            weighted[step, pl.ds(piece * width, width)] = (
                values * padded_weight[...] * scale
            ).astype(weighted.dtype)

    def weigh_rest():
        for step in (1, 3, 0):
            weigh(step)

    def gram(step, unit, part):
        start = pl.multiple_of(part * half, half)
        return jnp.dot(
            weighted[step, pl.ds(start, half)],
            partner[unit],
            preferred_element_type=jnp.float32,
        )

    weigh(2)

    @pl.when(seconds)
    def _():
        weigh_rest()

    def of_this(values):
        def pick(part):
            return jnp.where(
                y == 3,
                jnp.where(core == 0, values[1][0][part], values[1][1][part]),
                jnp.where(core == 0, values[0][0][part], values[0][1][part]),
            )

        return lambda part: jnp.where(part == 0, pick(0), pick(1))

    def tabulate(work):
        return [[[work(of) for of in halves] for halves in cores] for cores in PAIR_FIRST]

    def pair_first(unit, part):
        def among(of):
            return sum([jnp.where(unit == u, 1, 0) for u in of], 0 * unit)

        return of_this(tabulate(among))(part) == 1

    def relay_steps(t):
        for slot in range(units // 4):
            at = jnp.where(y == 1, RELAY_AT[1][slot], jnp.where(y == 2, RELAY_AT[2][slot], RELAY_AT[3][slot]))

            @pl.when((core == 1 - slot // (CHUNKS // 4)) & (y != 0) & (t == at))
            def _():
                relay_on(slot)

            @pl.when((core == 1 - slot // (CHUNKS // 4)) & (y == 2) & (t == AGAIN_AT[slot]))
            def _():
                relay_again(slot)

    def first_copy(job, way):
        return send(
            first_out.at[job, way],
            first_in.at[job, way],
            first_send.at[way, job],
            first_recv.at[way, job],
            (right, left)[way],
        )

    def second_copy(job, way):
        return send(
            second_out.at[job, way],
            second_in.at[job, way],
            second_send.at[way, job],
            second_recv.at[way, job],
            (right, left)[way],
        )

    def pair_copy(unit):
        return send(
            pair_out.at[unit], pair_in.at[unit], pair_send.at[unit], pair_recv.at[unit], mate
        )

    def early_copy(at):
        return send(
            early_out.at[at], early_in.at[at], early_send.at[at], early_recv.at[at], mate
        )

    def early_at(unit, step, part):
        def rank(of):
            return sum([jnp.where(unit > u, 1, 0) for u in of], 0 * unit)

        return of_this(tabulate(rank))(part) * RING + step

    def store(unit):
        column = pl.multiple_of(lax.rem(unit, CHUNKS) * width, width)
        return pltpu.make_async_copy(
            pair_in.at[unit],
            out_ref.at[unit // CHUNKS, :, pl.ds(column, width)],
            store_sem.at[unit],
        )

    def forward(unit):
        return send(
            block(partner, unit),
            block(partner, unit + CHUNKS),
            block_send.at[2 * CHUNKS + unit],
            block_recv.at[unit + CHUNKS],
            twin,
        )

    def job_of(kind, stage):
        late = kind == 2
        unit = stage - jnp.where(late, LAG, 0)
        mine = jnp.where(kind > 0, 1, 0)
        part = jnp.where(kind > 0, z_lo, 1 - z_lo)
        active = (unit >= 0) & (unit < units) & (pair_first(unit, part) == late)
        return late, unit, mine, part, active

    def each_kind(stage, work):
        def one(kind, carry):
            late, unit, mine, part, active = job_of(kind, stage)

            @pl.when(active)
            def _():
                work(late, unit, mine, part, unit * 2 + mine)

            return carry

        lax.fori_loop(0, 3, one, 0)

    def paired(late, unit, step, part):
        at = jnp.where(late, early_at(unit, step, part), early_in.shape[0] - 1)

        @pl.when(late)
        def _():
            early_copy(at).wait_recv()

        return gram(step, unit, part) + early_in[at].astype(jnp.float32)

    def first_step(late, unit, mine, part, job):
        value = paired(late, unit, 2, part).astype(first_out.dtype)
        for way in range(2):
            first_out[job, way] = value[way * quarter : (way + 1) * quarter]
            first_copy(job, way).start()

    def second_step(late, unit, mine, part, job):
        for way in range(2):
            value = paired(late, unit, (1, 3)[way], part)
            first_copy(job, way).wait_recv()
            joined = slice(way * quarter, (way + 1) * quarter)
            plain = slice((1 - way) * quarter, (2 - way) * quarter)
            second_out[job, way, joined] = (
                value[joined] + first_in[job, way].astype(jnp.float32)
            ).astype(second_out.dtype)
            second_out[job, way, plain] = value[plain].astype(second_out.dtype)
            second_copy(job, way).start()

    def third_step(late, unit, mine, part, job):
        value = paired(late, unit, 0, part)
        for way in range(2):
            second_copy(job, way).wait_recv()
        value = (
            value
            + second_in[job, 0].astype(jnp.float32)
            + second_in[job, 1].astype(jnp.float32)
        )

        @pl.when(mine == 0)
        def _():
            pair_out[unit] = value.astype(pair_out.dtype)
            pair_copy(unit).start()

        @pl.when((mine == 1) & jnp.logical_not(late))
        def _():
            total[unit] = value

        @pl.when(late)
        def _():
            pair_in[unit] = value.astype(pair_in.dtype)
            store(unit).start()

    def last_step(unit):
        pair_copy(unit).wait_recv()
        pair_in[unit] = (total[unit] + pair_in[unit].astype(jnp.float32)).astype(pair_in.dtype)
        store(unit).start()

    def step(t, carry):
        @pl.when(t < units)
        def _():
            send(
                block(partner, t), block(partner, t), block_send.at[0], block_recv.at[t], twin
            ).wait_recv()

            @pl.when(seconds & (t < CHUNKS))
            def _():
                forward(t).start()

            @pl.when(pair_first(t, 1 - z_lo))
            def _():
                def early(i, carry):
                    toward = lax.rem(i + 2, RING)
                    at = early_at(t, toward, 1 - z_lo)
                    early_out[at] = gram(toward, t, 1 - z_lo).astype(early_out.dtype)
                    early_copy(at).start()
                    return carry

                lax.fori_loop(0, RING, early, 0)

        each_kind(t, first_step)

        @pl.when((core == 0) & (t == 0))
        def _():
            weigh_rest()

        for j in range(CHUNKS):

            @pl.when(seconds & (t == jnp.where(y == 0, WRAP_AT[j], PASS_AT[j])))
            def _():
                pass_on(j, CHUNKS + j, block_send.at[CHUNKS + j])

        relay_steps(t)
        each_kind(t - STAGES[0], second_step)
        each_kind(t - STAGES[1], third_step)
        unit = t - STAGES[2]

        @pl.when((unit >= 0) & (unit < units) & jnp.logical_not(pair_first(unit, z_lo)))
        def _():
            last_step(unit)

        return carry

    relay_steps(-1)
    lax.fori_loop(0, ITERATIONS, step, 0)

    def finish(unit, carry):
        store(unit).wait()
        ahead = pair_first(unit, 1 - z_lo)

        @pl.when(ahead)
        def _():
            for toward in range(RING):
                early_copy(early_at(unit, toward, 1 - z_lo)).wait_send()

        @pl.when(jnp.logical_not(ahead))
        def _():
            pair_copy(unit).wait_send()
            for way in range(2):
                first_copy(unit * 2, way).wait_send()
                second_copy(unit * 2, way).wait_send()

        for way in range(2):
            first_copy(unit * 2 + 1, way).wait_send()
            second_copy(unit * 2 + 1, way).wait_send()
        return carry

    lax.fori_loop(0, units, finish, 0)

    def sent(at):
        send(
            block(own, 0), block(partner, 0), block_send.at[at], block_recv.at[0], twin
        ).wait_send()

    for j in range(CHUNKS):
        sent(j)

        @pl.when(seconds)
        def _():
            sent(CHUNKS + j)
            sent(2 * CHUNKS + j)

    for slot in range(units // 4):

        @pl.when((core == 1 - slot // (CHUNKS // 4)) & (y != 0))
        def _():
            sent(3 * CHUNKS + slot)

        @pl.when((core == 1 - slot // (CHUNKS // 4)) & (y == 2))
        def _():
            sent(3 * CHUNKS + units // 4 + slot)


def on_device(interactions, user_weight):
    users, items = interactions.shape
    slabs = lax.axis_size("slab")
    width, rows = items // CHUNKS, items // RING
    half = rows // 2
    units = ROUNDS * CHUNKS
    jobs, early = 2 * units, EARLY * RING
    half_type = interactions.dtype
    dma = pltpu.SemaphoreType.DMA
    tiles = pl.pallas_call(
        kernel,
        name="gram_tiles",
        out_shape=jax.ShapeDtypeStruct((ROUNDS, items // slabs, items), half_type),
        in_specs=[
            pl.BlockSpec(memory_space=pl.ANY),
            pl.BlockSpec(memory_space=pltpu.VMEM),
        ],
        out_specs=pl.BlockSpec(memory_space=pl.ANY),
        scratch_shapes=[
            pltpu.VMEM((1, PADDED), jnp.float32),
            pltpu.VMEM((CHUNKS, PADDED, width), half_type),
            pltpu.VMEM((RING, rows, PADDED), half_type),
            pltpu.VMEM((units, PADDED, width), half_type),
            pltpu.VMEM((units // 4, users, width), half_type),
            pltpu.VMEM((units // 4, users, width), half_type),
            pltpu.VMEM((jobs, 2, half // 2, width), half_type),
            pltpu.VMEM((jobs, 2, half // 2, width), half_type),
            pltpu.VMEM((jobs, 2, half, width), half_type),
            pltpu.VMEM((jobs, 2, half, width), half_type),
            pltpu.VMEM((units, half, width), half_type),
            pltpu.VMEM((units, half, width), half_type),
            pltpu.VMEM((early, half, width), half_type),
            pltpu.VMEM((early + 1, half, width), half_type),
            pltpu.VMEM((units, half, width), jnp.float32),
            dma((CHUNKS,)),
            dma((3 * CHUNKS + units // 2,)),
            dma((units,)),
            dma((units // 4,)),
            dma((units // 4,)),
            dma((2, jobs)),
            dma((2, jobs)),
            dma((2, jobs)),
            dma((2, jobs)),
            dma((units,)),
            dma((units,)),
            dma((early,)),
            dma((early,)),
            dma((units,)),
        ],
        compiler_params=pltpu.CompilerParams(
            collective_id=0, has_side_effects=True, vmem_limit_bytes=62 << 20
        ),
        cost_estimate=pl.CostEstimate(
            flops=ROUNDS * 2 * items * items * users,
            bytes_accessed=users * items * 2 + ROUNDS * items // slabs * items * 2,
            transcendentals=0,
        ),
    )(interactions, user_weight.reshape(1, users))
    return tiles.astype(jnp.float32)


def solution(mesh):
    in_specs = (P("slab", "blk"), P("slab"))
    out_specs = P(None, ("blk", "slab"), None)
    return jax.shard_map(
        on_device, mesh=mesh, in_specs=in_specs, out_specs=out_specs, check_vma=False
    )
```
